32 devices in a mesh: groups: 1, seq: 32 (over z, y, x, core).
Axes of the slice: x: 2, y: 2, z: 4, core: 2. Of those that a mesh axis runs over, the one named last changes fastest.
Arguments:
- queries: bfloat16 [32, 8192], P(('groups', 'seq')), may hold values from -15 to 15
- shared_prompt_keys: bfloat16 [65536, 1024], P(('groups', 'seq')), may hold values from -6.1 to 6.1
- shared_prompt_values: bfloat16 [65536, 1024], P(('groups', 'seq')), may hold values from -6 to 6
- private_cached_keys: bfloat16 [32, 256, 1024], P(('groups', 'seq')), may hold values from -9.1 to 9.1
- private_cached_values: bfloat16 [32, 256, 1024], P(('groups', 'seq')), may hold values from -6 to 6
- token_keys: bfloat16 [32, 1024], P(('groups', 'seq')), may hold values from -12 to 12
- token_values: bfloat16 [32, 1024], P(('groups', 'seq')), may hold values from -6 to 6
- suffix_lengths: int32 [32], P(('groups', 'seq')), may hold values from 1 to 256, as said below
- block_prompts: int32 [4], P('groups'), may hold values from 0 to 3, as said below
- out_weight: bfloat16 [8192, 8192], P(None, 'seq'), may hold values from -0.0625 to 0.0625
Outputs:
- projected: bfloat16 [32, 8192], P(('groups', 'seq'))
The draws below stay inside these ranges and needn't reach their ends.
Inputs may be any that keep to these rules, and one draw needn't show every extreme that they name: `block_prompts`: no prompt is read by more than 2 blocks, and one prompt is read by exactly 2. `suffix_lengths`: some continuation has exactly 256 live slots.
All inputs are finite; a program needn't handle non-finite values.
Results may differ from the reference program's by a relative error of at most 0.0053.
Values may be sent and summed in bfloat16 or wider, within the bound.
A program may use at most 128 MiB of HBM per device.

```python
import math
import jax
import jax.numpy as jnp
from jax import lax

D = 8192
QUERY_HEADS = 64
KEY_VALUE_HEADS = 8
HEAD_SIZE = 128
PROMPT_COUNT = 4
PROMPT_PER_UNIT = 2048
SUFFIX_SLOTS = 256
PROMPT_LENGTH = 16384
CONTINUATIONS = 32
ROWS_PER_BLOCK = 8
NB = 4
MOST = 2
N_SEQ = 32


def draw_queries(key, part):
    key = jax.random.fold_in(key, 1)
    sampled_items = 2.5 * jnp.clip(jax.random.normal(key, (CONTINUATIONS, D), jnp.float32), -6.0, 6.0)
    return sampled_items.astype(jnp.bfloat16)


def draw_shared_prompt_keys(key, part):
    key = jax.random.fold_in(key, 2)
    random_noise_key = jax.random.fold_in(key, 0)
    rows_overall = PROMPT_COUNT * PROMPT_LENGTH
    sampled_items = jnp.clip(jax.random.normal(random_noise_key, (rows_overall, KEY_VALUE_HEADS * HEAD_SIZE), jnp.float32), -6.0, 6.0)
    return sampled_items.astype(jnp.bfloat16)


def draw_private_cached_keys(key, part):
    key = jax.random.fold_in(key, 3)
    random_noise_key = jax.random.fold_in(key, 0)
    sampled_items = 1.5 * jnp.clip(jax.random.normal(random_noise_key, (CONTINUATIONS, SUFFIX_SLOTS, KEY_VALUE_HEADS * HEAD_SIZE), jnp.float32), -6.0, 6.0)
    return sampled_items.astype(jnp.bfloat16)


def draw_token_keys(key, part):
    key = jax.random.fold_in(key, 4)
    random_noise_key = jax.random.fold_in(key, 0)
    sampled_items = 2.0 * jnp.clip(jax.random.normal(random_noise_key, (CONTINUATIONS, KEY_VALUE_HEADS * HEAD_SIZE), jnp.float32), -6.0, 6.0)
    return sampled_items.astype(jnp.bfloat16)


def draw_suffix_lengths(key, part):
    key = jax.random.fold_in(key, 5)
    first_key, second_key = jax.random.split(key)
    lengths = jax.random.randint(first_key, (CONTINUATIONS,), 1, SUFFIX_SLOTS + 1)
    longest = jax.random.randint(second_key, (), 0, CONTINUATIONS)
    lengths = jnp.where(jnp.arange(CONTINUATIONS) == longest, SUFFIX_SLOTS, lengths)
    return lengths.astype(jnp.int32)


def draw_block_prompts(key, part):
    key = jax.random.fold_in(key, 6)
    first_key, second_key, third_key = jax.random.split(key, 3)
    order = jax.random.permutation(first_key, PROMPT_COUNT)
    seats = (PROMPT_COUNT - 1) * MOST
    others = order[1 + jnp.arange(seats) % max(PROMPT_COUNT - 1, 1)]
    others = others[jax.random.permutation(second_key, seats)]
    assigned = jnp.concatenate([jnp.full((MOST,), order[0]), others[:NB - MOST]])
    return assigned[jax.random.permutation(third_key, NB)].astype(jnp.int32)


def level_of(own_key, shape, pieces, low, top_value):
    def one(axis_at, shards_of):
        draws = jax.random.uniform(jax.random.fold_in(jax.random.fold_in(own_key, 6), axis_at), (shards_of,), jnp.float32, low / len(pieces), top_value / len(pieces))
        return jnp.repeat(jnp.exp(draws), shape[axis_at] // shards_of).reshape((-1,) + (1,) * (len(shape) - axis_at - 1))

    level = one(*pieces[0])
    for cut in pieces[1:]:
        level = level * one(*cut)
    return level


def normal_values(key, shape, width, bound, shards=(), kind=jnp.bfloat16):
    result = width * jax.random.normal(key, shape, jnp.float32)
    if shards:
        result = result * level_of(key, shape, shards, -0.22, 0.18)
    return jnp.clip(result, -bound, bound).astype(kind)


def setup_inputs(seed: int = 0, part: int = 0) -> dict:
    seeds = jax.random.split(jax.random.key(seed), 11)
    part_keys = jax.random.split(jax.random.fold_in(seeds[10], part), 11)
    queries = draw_queries(jax.random.fold_in(jax.random.fold_in(seeds[10], part), 71), part)
    shared_prompt_keys = draw_shared_prompt_keys(jax.random.fold_in(jax.random.fold_in(seeds[10], part), 71), part)
    shared_prompt_values = normal_values(part_keys[2], (PROMPT_COUNT * PROMPT_LENGTH, KEY_VALUE_HEADS * HEAD_SIZE), 1.0, 6.0, ((0, 32),))
    private_cached_keys = draw_private_cached_keys(jax.random.fold_in(jax.random.fold_in(seeds[10], part), 71), part)
    private_cached_values = normal_values(part_keys[4], (CONTINUATIONS, SUFFIX_SLOTS, KEY_VALUE_HEADS * HEAD_SIZE), 1.0, 6.0, ((0, 32),))
    token_keys = draw_token_keys(jax.random.fold_in(jax.random.fold_in(seeds[10], part), 71), part)
    token_values = normal_values(part_keys[6], (CONTINUATIONS, KEY_VALUE_HEADS * HEAD_SIZE), 1.0, 6.0, ((0, 32),))
    suffix_lengths = draw_suffix_lengths(jax.random.fold_in(jax.random.fold_in(seeds[10], part), 71), part)
    block_prompts = draw_block_prompts(jax.random.fold_in(jax.random.fold_in(seeds[10], part), 71), part)
    out_weight = normal_values(seeds[9], (D, D), D ** -0.5, 0.0625, ((1, 32),))
    return {"queries": queries, "shared_prompt_keys": shared_prompt_keys, "shared_prompt_values": shared_prompt_values, "private_cached_keys": private_cached_keys, "private_cached_values": private_cached_values, "token_keys": token_keys, "token_values": token_values, "suffix_lengths": suffix_lengths, "block_prompts": block_prompts, "out_weight": out_weight}


masked_score = -1e+30

def prompt_piece(rows_of_queries, keys_block, values_block):
    score_scale = 1.0 / math.sqrt(HEAD_SIZE)
    scores = jnp.einsum('rkgd,pkd->rkgp', rows_of_queries, keys_block) * score_scale
    row_max = lax.optimization_barrier(jnp.max(scores, axis=3))
    weights = jnp.exp(scores - row_max[..., None])
    rows_overall = lax.optimization_barrier(jnp.sum(weights, axis=3))
    rounded = lax.optimization_barrier(weights.astype(jnp.bfloat16)).astype(jnp.float32)
    head_part = jnp.einsum('rkgp,pkd->rkgd', rounded, values_block) / rows_overall[..., None]
    return (row_max, rows_overall, head_part.astype(jnp.bfloat16))

def reference(queries, shared_prompt_keys, shared_prompt_values, private_cached_keys, private_cached_values, token_keys, token_values, suffix_lengths, block_prompts, out_weight):
    query_group_count = QUERY_HEADS // KEY_VALUE_HEADS
    prompt_segment = N_SEQ // PROMPT_COUNT
    blocks = queries.shape[0] // ROWS_PER_BLOCK
    score_scale = 1.0 / math.sqrt(HEAD_SIZE)

    def one_block(block_index):
        leading_row = (block_index * ROWS_PER_BLOCK).astype(jnp.int32)
        rows_of_queries = lax.dynamic_slice_in_dim(queries, leading_row, ROWS_PER_BLOCK, 0).astype(jnp.float32).reshape(ROWS_PER_BLOCK, KEY_VALUE_HEADS, query_group_count, HEAD_SIZE)
        prompt = block_prompts[block_index]
        prompt_offset = (prompt * PROMPT_LENGTH).astype(jnp.int32)
        joined_keys = lax.dynamic_slice_in_dim(shared_prompt_keys, prompt_offset, PROMPT_LENGTH, 0).reshape(prompt_segment, PROMPT_PER_UNIT, KEY_VALUE_HEADS, HEAD_SIZE)
        joined_values = lax.dynamic_slice_in_dim(shared_prompt_values, prompt_offset, PROMPT_LENGTH, 0).reshape(prompt_segment, PROMPT_PER_UNIT, KEY_VALUE_HEADS, HEAD_SIZE)

        def one_piece(key_pair):
            return prompt_piece(rows_of_queries, key_pair[0].astype(jnp.float32), key_pair[1].astype(jnp.float32))
        prompt_max, prompt_total, prompt_part = lax.map(one_piece, (joined_keys, joined_values))
        continuation_keys = lax.dynamic_slice_in_dim(private_cached_keys, leading_row, ROWS_PER_BLOCK, 0)
        continuation_values = lax.dynamic_slice_in_dim(private_cached_values, leading_row, ROWS_PER_BLOCK, 0)
        latest_key = lax.dynamic_slice_in_dim(token_keys, leading_row, ROWS_PER_BLOCK, 0)
        latest_value = lax.dynamic_slice_in_dim(token_values, leading_row, ROWS_PER_BLOCK, 0)
        cached_key_rows = jnp.concatenate([continuation_keys, latest_key[:, None, :]], axis=1).astype(jnp.float32).reshape(ROWS_PER_BLOCK, SUFFIX_SLOTS + 1, KEY_VALUE_HEADS, HEAD_SIZE)
        cached_value_rows = jnp.concatenate([continuation_values, latest_value[:, None, :]], axis=1).astype(jnp.float32).reshape(ROWS_PER_BLOCK, SUFFIX_SLOTS + 1, KEY_VALUE_HEADS, HEAD_SIZE)
        lengths = lax.dynamic_slice_in_dim(suffix_lengths, leading_row, ROWS_PER_BLOCK, 0)
        positions = jnp.arange(SUFFIX_SLOTS + 1, dtype=jnp.int32)
        live_keys = (positions[None, :] < lengths[:, None]) | (positions[None, :] == SUFFIX_SLOTS)
        scores = jnp.einsum('rkgd,rskd->rkgs', rows_of_queries, cached_key_rows) * score_scale
        scores = jnp.where(live_keys[:, None, None, :], scores, masked_score)
        suffix_max = lax.optimization_barrier(jnp.max(scores, axis=3))
        weights = jnp.exp(scores - suffix_max[..., None])
        suffix_total = lax.optimization_barrier(jnp.sum(weights, axis=3))
        rounded = lax.optimization_barrier(weights.astype(jnp.bfloat16)).astype(jnp.float32)
        suffix_part = jnp.einsum('rkgs,rskd->rkgd', rounded, cached_value_rows) / suffix_total[..., None]
        row_best = jnp.maximum(suffix_max, lax.optimization_barrier(jnp.max(prompt_max, axis=0)))
        factor = prompt_total * jnp.exp(prompt_max - row_best[None])
        own_factor = suffix_total * jnp.exp(suffix_max - row_best)
        numerator = own_factor[..., None] * suffix_part + lax.optimization_barrier(jnp.sum(factor[..., None] * prompt_part.astype(jnp.float32), axis=0))
        denominator = own_factor + lax.optimization_barrier(jnp.sum(factor, axis=0))
        return (numerator / denominator[..., None]).astype(jnp.bfloat16).reshape(ROWS_PER_BLOCK, QUERY_HEADS * HEAD_SIZE)
    attention = lax.map(one_block, jnp.arange(blocks, dtype=jnp.int32)).reshape(blocks * ROWS_PER_BLOCK, QUERY_HEADS * HEAD_SIZE)
    return jnp.dot(attention, out_weight, preferred_element_type=jnp.float32).astype(jnp.bfloat16)
```

```python
import functools
import math

import jax
import jax.numpy as jnp
from jax import lax
from jax.experimental import pallas as pl
from jax.experimental.pallas import tpu as pltpu
from jax.sharding import PartitionSpec as P

QUERY_HEADS = 64
KEY_VALUE_HEADS = 8
GROUP = QUERY_HEADS // KEY_VALUE_HEADS
HEAD_SIZE = 128
PROMPT_COUNT = 4
SLOTS = 2
SCALE = 1.0 / math.sqrt(HEAD_SIZE)
SCALE_LOG2 = SCALE * math.log2(math.e)
VMEM = pl.BlockSpec(memory_space=pltpu.VMEM)
SMEM = pl.BlockSpec(memory_space=pltpu.SMEM)
NT = (((1,), (1,)), ((), ()))


def place(segment):
    me = lax.axis_index("seq")
    return me // segment, lax.rem(me, segment)


def each(count, step):
    def one(i, carry):
        step(i + 1)
        return carry

    lax.fori_loop(0, count - 1, one, 0)


def barrier(segment):
    z, j = place(segment)
    sem = pltpu.get_barrier_semaphore()

    def plane(d):
        to = z * segment + lax.rem(j + d, segment)
        pl.semaphore_signal(sem, inc=1, device_id={"seq": to})

    def column(d):
        to = lax.rem(z + d, PROMPT_COUNT) * segment + j
        pl.semaphore_signal(sem, inc=1, device_id={"seq": to})

    each(segment, plane)
    each(PROMPT_COUNT, column)
    pl.semaphore_wait(sem, segment - 1 + PROMPT_COUNT - 1)


def exchange(ref, send, recv, segment, source=None, in_plane=True):
    z, j = place(segment)
    count, mine = (segment, j) if in_plane else (PROMPT_COUNT, z)

    def copy(d, block):
        peer = lax.rem(mine + d, count)
        to = z * segment + peer if in_plane else peer * segment + j
        src = ref.at[mine] if source is None else source.at[peer]
        return pltpu.make_async_remote_copy(
            src_ref=src,
            dst_ref=ref.at[block],
            send_sem=send.at[d],
            recv_sem=recv.at[block],
            device_id={"seq": to},
        )

    def start():
        each(count, lambda d: copy(d, mine).start())

    def wait_recv():
        each(count, lambda d: copy(d, lax.rem(mine + d, count)).wait_recv())

    def wait_send():
        each(count, lambda d: copy(d, mine).wait_send())

    return start, wait_recv, wait_send


def lanes(shape):
    return lax.broadcasted_iota(jnp.int32, shape, len(shape) - 1)


def pick(at, choices):
    at = jnp.full(choices[0].shape, at, jnp.int32)
    out = choices[0]
    for i, choice in enumerate(choices[1:]):
        out = jnp.where(at == i + 1, choice, out)
    return out


def own_suffix(length, q, keys_ref, values_ref, key_ref, value_ref):
    parts = []
    logs = jnp.zeros((GROUP, 128), jnp.float32)
    slots = keys_ref.shape[0]
    live = lanes((GROUP, slots)) < length
    for k in range(KEY_VALUE_HEADS):
        cut = slice(k * HEAD_SIZE, (k + 1) * HEAD_SIZE)
        head = q[k * GROUP : (k + 1) * GROUP]
        scores = lax.dot_general(
            head.astype(jnp.bfloat16), keys_ref[:, cut], NT, preferred_element_type=jnp.float32
        )
        scores = jnp.where(live, scores * SCALE, -1e30)
        fresh = jnp.sum(head * key_ref[:, cut].astype(jnp.float32), axis=1, keepdims=True) * SCALE
        top = jnp.maximum(jnp.max(scores, axis=1, keepdims=True), fresh)
        weights = jnp.exp(scores - top)
        fresh_weight = jnp.exp(fresh - top)
        total = jnp.sum(weights, axis=1, keepdims=True) + fresh_weight
        out = jnp.dot(
            weights.astype(jnp.bfloat16), values_ref[:, cut], preferred_element_type=jnp.float32
        )
        fresh_weight = fresh_weight.astype(jnp.bfloat16).astype(jnp.float32)
        out = out + fresh_weight * value_ref[:, cut].astype(jnp.float32)
        parts.append(out / total)
        logs = jnp.where(lanes(logs.shape) == k, top + jnp.log(total), logs)
    return jnp.concatenate(parts, axis=0), logs


def gather_kernel(
    segment,
    slot_ref,
    length_ref,
    q_ref,
    keys_ref,
    values_ref,
    key_ref,
    value_ref,
    out_ref,
    part_ref,
    logs_ref,
    column,
    sems,
):
    z, j = place(segment)
    barrier(segment)
    column[z] = q_ref[...]
    start, recv, sent = exchange(column, sems.at[0], sems.at[1], segment, in_plane=False)
    start()
    part, logs = own_suffix(
        length_ref[0], q_ref[...].astype(jnp.float32), keys_ref, values_ref, key_ref, value_ref
    )
    part_ref[z] = part.astype(jnp.bfloat16)
    logs_ref[z] = logs
    recv()
    for s in range(SLOTS):
        out_ref[j, s] = pick(slot_ref[s], [column[b] for b in range(PROMPT_COUNT)])
    start2, recv2, sent2 = exchange(out_ref, sems.at[2], sems.at[3], segment)
    start3, recv3, sent3 = exchange(part_ref, sems.at[4], sems.at[5], segment, in_plane=False)
    start4, recv4, sent4 = exchange(logs_ref, sems.at[6], sems.at[7], segment, in_plane=False)
    start2()
    start3()
    start4()
    for wait in (recv2, recv3, recv4, sent, sent2, sent3, sent4):
        wait()


def attend_kernel(q_ref, keys_ref, values_ref, part_ref, logs_ref):
    step = pl.program_id(0)
    segment = q_ref.shape[0]
    rows = segment * SLOTS * GROUP

    @pl.when(step == 0)
    def _():
        logs_ref[...] = jnp.zeros_like(logs_ref)

    q = q_ref[...].astype(jnp.float32).reshape(segment * SLOTS, 2, GROUP, HEAD_SIZE)
    parts = []
    logs = logs_ref[...]
    for h in range(2):
        cut = slice(h * HEAD_SIZE, (h + 1) * HEAD_SIZE)
        head = q[:, h].reshape(rows, HEAD_SIZE).astype(jnp.bfloat16)
        scores = lax.dot_general(head, keys_ref[:, cut], NT, preferred_element_type=jnp.float32)
        top = jnp.max(scores, axis=1, keepdims=True)
        weights = jnp.exp2((scores - top) * SCALE_LOG2)
        total = jnp.sum(weights, axis=1, keepdims=True)
        out = jnp.dot(
            weights.astype(jnp.bfloat16), values_ref[:, cut], preferred_element_type=jnp.float32
        )
        parts.append((out / total).reshape(segment * SLOTS, GROUP, HEAD_SIZE))
        logs = jnp.where(lanes(logs.shape) == step * 2 + h, top * SCALE + jnp.log(total), logs)
    logs_ref[...] = logs
    both = jnp.concatenate(parts, axis=1)
    part_ref[...] = both.astype(jnp.bfloat16).reshape(part_ref.shape)


def spread(weights, pair):
    first = weights[:, 2 * pair : 2 * pair + 1]
    second = weights[:, 2 * pair + 1 : 2 * pair + 2]
    return jnp.concatenate([first, second], axis=0)


def combine_kernel(
    segment,
    index_ref,
    parts_ref,
    logs_ref,
    suffix_ref,
    suffix_logs_ref,
    out_ref,
    got,
    got_logs,
    column,
    column_logs,
    sems,
):
    z, j = place(segment)
    barrier(segment)
    first = exchange(got, sems.at[0], sems.at[1], segment, source=parts_ref)
    first_logs = exchange(got_logs, sems.at[2], sems.at[3], segment, source=logs_ref)
    first[0]()
    first_logs[0]()
    got[j] = parts_ref[j]
    got_logs[j] = logs_ref[j]
    first_logs[1]()
    logs = got_logs[...]
    best = jnp.max(logs, axis=0)
    weights = jnp.exp(logs - best[None])
    total = jnp.sum(weights, axis=0)
    weights = weights / total[None]
    column_logs[z] = best + jnp.log(total)
    first[1]()
    for s in range(SLOTS):
        for pair in range(KEY_VALUE_HEADS // 2):
            rows = slice(pair * 16, pair * 16 + 16)
            acc = jnp.zeros((16, HEAD_SIZE), jnp.float32)
            for i in range(segment):
                w = spread(weights[i, s * GROUP : (s + 1) * GROUP], pair)
                acc = acc + w * got[i, s, rows].astype(jnp.float32)
            column[z, s, rows] = acc.astype(jnp.bfloat16)
    second = exchange(column, sems.at[4], sems.at[5], segment, in_plane=False)
    second_logs = exchange(column_logs, sems.at[6], sems.at[7], segment, in_plane=False)
    second[0]()
    second_logs[0]()
    second_logs[1]()
    second[1]()
    for b in range(PROMPT_COUNT):
        at = index_ref[b]
        prompt = pick(at, [column[i // SLOTS, i % SLOTS] for i in range(PROMPT_COUNT * SLOTS)])
        prompt = prompt.astype(jnp.float32)
        prompt_logs = pick(
            at,
            [
                column_logs[p, s * GROUP : (s + 1) * GROUP]
                for p in range(PROMPT_COUNT)
                for s in range(SLOTS)
            ],
        )
        own_logs = suffix_logs_ref[b]
        best = jnp.maximum(prompt_logs, own_logs)
        prompt_weight = jnp.exp(prompt_logs - best)
        own_weight = jnp.exp(own_logs - best)
        total = prompt_weight + own_weight
        prompt_weight = prompt_weight / total
        own_weight = own_weight / total
        for pair in range(KEY_VALUE_HEADS // 2):
            rows = slice(pair * 16, pair * 16 + 16)
            row = spread(prompt_weight, pair) * prompt[rows]
            row = row + spread(own_weight, pair) * suffix_ref[b, rows].astype(jnp.float32)
            out_ref[j, b, rows] = row.astype(jnp.bfloat16)
    third = exchange(out_ref, sems.at[8], sems.at[9], segment)
    third[0]()
    third[1]()
    for group in (first, first_logs, second, second_logs, third):
        group[2]()


def body(
    queries,
    shared_prompt_keys,
    shared_prompt_values,
    private_cached_keys,
    private_cached_values,
    token_keys,
    token_values,
    suffix_lengths,
    block_prompts,
    out_weight,
):
    n = lax.axis_size("seq")
    segment = n // PROMPT_COUNT
    z, j = place(segment)
    count, width = queries.shape
    assert count == 1 and block_prompts.shape[0] == PROMPT_COUNT
    heads, size = QUERY_HEADS, HEAD_SIZE
    positions = shared_prompt_keys.shape[0]
    bf, f32 = jnp.bfloat16, jnp.float32
    shape = jax.ShapeDtypeStruct

    blocks = jnp.arange(PROMPT_COUNT, dtype=jnp.int32)
    same = block_prompts[:, None] == block_prompts[None, :]
    rank = jnp.sum(same & (blocks[None, :] < blocks[:, None]), axis=1).astype(jnp.int32)
    mine = (block_prompts[None, :] == z) & (rank[None, :] == blocks[:SLOTS, None])
    slot_block = jnp.sum(jnp.where(mine, blocks[None, :], 0), axis=1).astype(jnp.int32)
    index = block_prompts * SLOTS + rank

    most = max(segment, PROMPT_COUNT)
    gathered, suffix, suffix_logs = pl.pallas_call(
        functools.partial(gather_kernel, segment),
        out_shape=(
            shape((segment, SLOTS, heads, size), bf),
            shape((PROMPT_COUNT, heads, size), bf),
            shape((PROMPT_COUNT, GROUP, 128), f32),
        ),
        in_specs=[SMEM, SMEM] + [VMEM] * 5,
        out_specs=(VMEM, VMEM, VMEM),
        scratch_shapes=[
            pltpu.VMEM((PROMPT_COUNT, heads, size), bf),
            pltpu.SemaphoreType.DMA((8, most)),
        ],
        compiler_params=pltpu.CompilerParams(
            collective_id=0, has_side_effects=True, vmem_limit_bytes=24 << 20
        ),
    )(
        slot_block,
        suffix_lengths,
        queries.reshape(heads, size),
        private_cached_keys[0],
        private_cached_values[0],
        token_keys,
        token_values,
    )

    rows = segment * SLOTS * GROUP
    parts, logs = pl.pallas_call(
        attend_kernel,
        out_shape=(shape((segment, SLOTS, heads, size), bf), shape((rows, 128), f32)),
        grid=(KEY_VALUE_HEADS // 2,),
        in_specs=[
            pl.BlockSpec((segment, SLOTS, 16, size), lambda i: (0, 0, i, 0)),
            pl.BlockSpec((positions, 2 * size), lambda i: (0, i)),
            pl.BlockSpec((positions, 2 * size), lambda i: (0, i)),
        ],
        out_specs=(
            pl.BlockSpec((segment, SLOTS, 16, size), lambda i: (0, 0, i, 0)),
            pl.BlockSpec((rows, 128), lambda i: (0, 0)),
        ),
        compiler_params=pltpu.CompilerParams(vmem_limit_bytes=44 << 20),
    )(gathered, shared_prompt_keys, shared_prompt_values)

    attention = pl.pallas_call(
        functools.partial(combine_kernel, segment),
        out_shape=shape((segment, PROMPT_COUNT, heads, size), bf),
        in_specs=[SMEM] + [VMEM] * 4,
        out_specs=VMEM,
        scratch_shapes=[
            pltpu.VMEM((segment, SLOTS, heads, size), bf),
            pltpu.VMEM((segment, SLOTS * GROUP, 128), f32),
            pltpu.VMEM((PROMPT_COUNT, SLOTS, heads, size), bf),
            pltpu.VMEM((PROMPT_COUNT, SLOTS * GROUP, 128), f32),
            pltpu.SemaphoreType.DMA((10, most)),
        ],
        compiler_params=pltpu.CompilerParams(
            collective_id=1, has_side_effects=True, vmem_limit_bytes=24 << 20
        ),
    )(index, parts, logs.reshape(segment, SLOTS * GROUP, 128), suffix, suffix_logs)

    panel = jnp.dot(
        attention.reshape(n, width), out_weight, preferred_element_type=f32
    ).astype(bf)
    panel = panel.reshape(segment, PROMPT_COUNT, -1).transpose(1, 0, 2).reshape(n, -1)
    return lax.all_to_all(panel, "seq", split_axis=0, concat_axis=1, tiled=True)


def solution(mesh):
    in_specs = (
        P(("groups", "seq"), None),
        P(("groups", "seq"), None),
        P(("groups", "seq"), None),
        P(("groups", "seq"), None, None),
        P(("groups", "seq"), None, None),
        P(("groups", "seq"), None),
        P(("groups", "seq"), None),
        P(("groups", "seq")),
        P("groups"),
        P(None, "seq"),
    )
    out_specs = P(("groups", "seq"), None)
    return jax.shard_map(body, mesh=mesh, in_specs=in_specs, out_specs=out_specs, check_vma=False)
```

```python
import functools
import math

import jax
import jax.numpy as jnp
from jax import lax
from jax.experimental import pallas as pl
from jax.experimental.pallas import tpu as pltpu
from jax.sharding import PartitionSpec as P

QUERY_HEADS = 64
KEY_VALUE_HEADS = 8
GROUP = QUERY_HEADS // KEY_VALUE_HEADS
HEAD_SIZE = 128
PROMPT_COUNT = 4
SLOTS = 2
SCALE = 1.0 / math.sqrt(HEAD_SIZE)
SCALE_LOG2 = SCALE * math.log2(math.e)
VMEM = pl.BlockSpec(memory_space=pltpu.VMEM)
ANY = pl.BlockSpec(memory_space=pl.ANY)
SMEM = pl.BlockSpec(memory_space=pltpu.SMEM)
NT = (((1,), (1,)), ((), ()))


def place(segment):
    me = lax.axis_index("seq")
    return me // segment, lax.rem(me, segment)


def each(count, step):
    def one(i, carry):
        step(i + 1)
        return carry

    lax.fori_loop(0, count - 1, one, 0)


def greet(segment):
    z, j = place(segment)
    sem = pltpu.get_barrier_semaphore()

    def plane(d):
        to = z * segment + lax.rem(j + d, segment)
        pl.semaphore_signal(sem, inc=1, device_id={"seq": to})

    def column(d):
        to = lax.rem(z + d, PROMPT_COUNT) * segment + j
        pl.semaphore_signal(sem, inc=1, device_id={"seq": to})

    each(segment, plane)
    each(PROMPT_COUNT, column)


def greeted(segment):
    pl.semaphore_wait(pltpu.get_barrier_semaphore(), segment - 1 + PROMPT_COUNT - 1)


def exchange(ref, send, recv, segment, source=None, in_plane=True, rows=None):
    z, j = place(segment)
    count, mine = (segment, j) if in_plane else (PROMPT_COUNT, z)

    def view(array, block):
        return array.at[block] if rows is None else array.at[block, :, rows]

    def copy(d, block):
        peer = lax.rem(mine + d, count)
        to = z * segment + peer if in_plane else peer * segment + j
        return pltpu.make_async_remote_copy(
            src_ref=view(ref, mine) if source is None else view(source, peer),
            dst_ref=view(ref, block),
            send_sem=send.at[d],
            recv_sem=recv.at[block],
            device_id={"seq": to},
        )

    def start():
        each(count, lambda d: copy(d, mine).start())

    def wait_recv():
        each(count, lambda d: copy(d, lax.rem(mine + d, count)).wait_recv())

    def wait_send():
        each(count, lambda d: copy(d, mine).wait_send())

    return start, wait_recv, wait_send


def lanes(shape):
    return lax.broadcasted_iota(jnp.int32, shape, len(shape) - 1)


def pick(at, choices):
    at = jnp.full(choices[0].shape, at, jnp.int32)
    out = choices[0]
    for i, choice in enumerate(choices[1:]):
        out = jnp.where(at == i + 1, choice, out)
    return out


def own_suffix(length, q, keys_ref, values_ref, key_ref, value_ref):
    parts = []
    logs = jnp.zeros((GROUP, 128), jnp.float32)
    slots = keys_ref.shape[0]
    live = lanes((GROUP, slots)) < length
    for k in range(KEY_VALUE_HEADS):
        cut = slice(k * HEAD_SIZE, (k + 1) * HEAD_SIZE)
        head = q[k * GROUP : (k + 1) * GROUP]
        scores = lax.dot_general(
            head.astype(jnp.bfloat16), keys_ref[:, cut], NT, preferred_element_type=jnp.float32
        )
        scores = jnp.where(live, scores * SCALE, -1e30)
        fresh = jnp.sum(head * key_ref[:, cut].astype(jnp.float32), axis=1, keepdims=True) * SCALE
        top = jnp.maximum(jnp.max(scores, axis=1, keepdims=True), fresh)
        weights = jnp.exp(scores - top)
        fresh_weight = jnp.exp(fresh - top)
        total = jnp.sum(weights, axis=1, keepdims=True) + fresh_weight
        out = jnp.dot(
            weights.astype(jnp.bfloat16), values_ref[:, cut], preferred_element_type=jnp.float32
        )
        fresh_weight = fresh_weight.astype(jnp.bfloat16).astype(jnp.float32)
        out = out + fresh_weight * value_ref[:, cut].astype(jnp.float32)
        parts.append(out / total)
        logs = jnp.where(lanes(logs.shape) == k, top + jnp.log(total), logs)
    return jnp.concatenate(parts, axis=0), logs


def spread(weights, pair):
    first = weights[:, 2 * pair : 2 * pair + 1]
    second = weights[:, 2 * pair + 1 : 2 * pair + 2]
    return jnp.concatenate([first, second], axis=0)


def pair_rows(i):
    return pl.ds(pl.multiple_of(i * 16, 16), 16)


def attend(i, segment, q_ref, keys_ref, values_ref, part_ref, logs_ref):
    rows = segment * SLOTS * GROUP
    q = q_ref[:, :, pair_rows(i), :].astype(jnp.float32)
    q = q.reshape(segment * SLOTS, 2, GROUP, HEAD_SIZE)
    parts = []
    logs = logs_ref[...].reshape(rows, 128)
    for h in range(2):
        cut = pl.ds(pl.multiple_of((i * 2 + h) * HEAD_SIZE, HEAD_SIZE), HEAD_SIZE)
        head = q[:, h].reshape(rows, HEAD_SIZE).astype(jnp.bfloat16)
        scores = lax.dot_general(head, keys_ref[:, cut], NT, preferred_element_type=jnp.float32)
        top = jnp.max(scores, axis=1, keepdims=True)
        weights = jnp.exp2((scores - top) * SCALE_LOG2)
        total = jnp.sum(weights, axis=1, keepdims=True)
        out = jnp.dot(
            weights.astype(jnp.bfloat16), values_ref[:, cut], preferred_element_type=jnp.float32
        )
        parts.append((out / total).reshape(segment * SLOTS, GROUP, HEAD_SIZE))
        logs = jnp.where(lanes(logs.shape) == i * 2 + h, top * SCALE + jnp.log(total), logs)
    logs_ref[...] = logs.reshape(logs_ref.shape)
    both = jnp.concatenate(parts, axis=1).astype(jnp.bfloat16)
    part_ref[:, :, pair_rows(i), :] = both.reshape(segment, SLOTS, 16, HEAD_SIZE)


def kernel(
    segment,
    prompts_ref,
    length_ref,
    q_ref,
    key_ref,
    value_ref,
    own_keys_hbm,
    own_values_hbm,
    keys_hbm,
    values_hbm,
    weight_hbm,
    out_ref,
    own_keys,
    own_values,
    keys,
    values,
    weight,
    q_column,
    q_all,
    suffix,
    suffix_logs,
    parts,
    logs,
    got,
    got_logs,
    column,
    column_logs,
    rows_all,
    rows_wide,
    panel,
    panel_column,
    panel_rows,
    local_sems,
    sems,
    chunk_sems,
):
    z, j = place(segment)
    n = segment * PROMPT_COUNT
    greet(segment)
    loads = [
        pltpu.make_async_copy(src, dst, local_sems.at[i])
        for i, (src, dst) in enumerate(
            (
                (own_keys_hbm, own_keys),
                (own_values_hbm, own_values),
                (keys_hbm, keys),
                (values_hbm, values),
                (weight_hbm, weight),
            )
        )
    ]
    for load in loads:
        load.start()

    flat = q_ref[...].astype(jnp.float32)
    q = jnp.concatenate(
        [flat[:, h * HEAD_SIZE : (h + 1) * HEAD_SIZE] for h in range(QUERY_HEADS)], axis=0
    )
    q_column[z] = q.astype(jnp.bfloat16)
    logs[...] = jnp.zeros_like(logs)
    prompts = [prompts_ref[b] for b in range(PROMPT_COUNT)]
    ranks = []
    for b in range(PROMPT_COUNT):
        rank = jnp.int32(0)
        for c in range(b):
            rank = rank + jnp.where(prompts[c] == prompts[b], 1, 0)
        ranks.append(rank)
    slot_block = []
    for s in range(SLOTS):
        block = jnp.int32(0)
        for b in range(PROMPT_COUNT):
            block = jnp.where((prompts[b] == z) & (ranks[b] == s), b, block)
        slot_block.append(block)

    greeted(segment)
    ask = exchange(q_column, sems.at[0], sems.at[1], segment, in_plane=False)
    ask[0]()
    loads[0].wait()
    loads[1].wait()
    part, own_logs = own_suffix(length_ref[0], q, own_keys, own_values, key_ref, value_ref)
    suffix[z] = part
    suffix_logs[z] = own_logs
    ask[1]()
    for s in range(SLOTS):
        q_all[j, s] = pick(slot_block[s], [q_column[b] for b in range(PROMPT_COUNT)])

    def ask_plane(i):
        return exchange(
            q_all, chunk_sems.at[0, i], chunk_sems.at[1, i], segment, rows=pair_rows(i)
        )

    def answer(i):
        return exchange(
            got,
            chunk_sems.at[2, i],
            chunk_sems.at[3, i],
            segment,
            source=parts,
            rows=pair_rows(i),
        )

    pairs = KEY_VALUE_HEADS // 2

    def all_pairs(step):
        def one(i, carry):
            step(i)
            return carry

        lax.fori_loop(0, pairs, one, 0)

    all_pairs(lambda i: ask_plane(i)[0]())
    tell = exchange(suffix, sems.at[2], sems.at[3], segment, in_plane=False)
    tell_logs = exchange(suffix_logs, sems.at[4], sems.at[5], segment, in_plane=False)
    tell[0]()
    tell_logs[0]()
    loads[2].wait()
    loads[3].wait()

    def work(i):
        ask_plane(i)[1]()
        attend(i, segment, q_all, keys, values, parts, logs)
        answer(i)[0]()

    all_pairs(work)
    answer_logs = exchange(got_logs, sems.at[6], sems.at[7], segment, source=logs)
    answer_logs[0]()
    got[j] = parts[j]
    got_logs[j] = logs[j]
    answer_logs[1]()
    all_logs = got_logs[...]
    best = jnp.max(all_logs, axis=0)
    weights = jnp.exp(all_logs - best[None])
    total = jnp.sum(weights, axis=0)
    weights = weights / total[None]
    column_logs[z] = best + jnp.log(total)
    all_pairs(lambda i: answer(i)[1]())
    for s in range(SLOTS):
        for pair in range(pairs):
            rows = slice(pair * 16, pair * 16 + 16)
            acc = jnp.zeros((16, HEAD_SIZE), jnp.float32)
            for i in range(segment):
                w = spread(weights[i, s * GROUP : (s + 1) * GROUP], pair)
                acc = acc + w * got[i, s, rows].astype(jnp.float32)
            column[z, s, rows] = acc.astype(jnp.bfloat16)
    share = exchange(column, sems.at[8], sems.at[9], segment, in_plane=False)
    share_logs = exchange(column_logs, sems.at[10], sems.at[11], segment, in_plane=False)
    share_logs[0]()
    share[0]()
    tell_logs[1]()
    tell[1]()
    share_logs[1]()
    share[1]()
    for b in range(PROMPT_COUNT):
        at = prompts[b] * SLOTS + ranks[b]
        prompt = pick(at, [column[i // SLOTS, i % SLOTS] for i in range(PROMPT_COUNT * SLOTS)])
        prompt = prompt.astype(jnp.float32)
        prompt_logs = pick(
            at,
            [
                column_logs[p, s * GROUP : (s + 1) * GROUP]
                for p in range(PROMPT_COUNT)
                for s in range(SLOTS)
            ],
        )
        own_logs = suffix_logs[b]
        best = jnp.maximum(prompt_logs, own_logs)
        prompt_weight = jnp.exp(prompt_logs - best)
        own_weight = jnp.exp(own_logs - best)
        total = prompt_weight + own_weight
        prompt_weight = prompt_weight / total
        own_weight = own_weight / total
        for pair in range(pairs):
            rows = slice(pair * 16, pair * 16 + 16)
            row = spread(prompt_weight, pair) * prompt[rows]
            row = row + spread(own_weight, pair) * suffix[b, rows]
            rows_all[j, b, rows] = row.astype(jnp.bfloat16)
    gather = exchange(rows_all, sems.at[12], sems.at[13], segment)
    gather[0]()
    loads[4].wait()
    gather[1]()

    def widen(i, carry):
        for b in range(PROMPT_COUNT):
            at = pl.multiple_of((b * segment + i) * QUERY_HEADS, QUERY_HEADS)
            rows_wide[pl.ds(at, QUERY_HEADS), :] = rows_all[i, b].astype(jnp.float32)
        return carry

    lax.fori_loop(0, segment, widen, 0)

    def project(i, acc):
        for pair in range(4):
            h = i * 8 + pair * 2
            both = [rows_wide[pl.ds(h + o, n, stride=QUERY_HEADS), :] for o in range(2)]
            left = jnp.concatenate(both, axis=1).astype(jnp.bfloat16)
            at = pl.multiple_of(h * HEAD_SIZE, 2 * HEAD_SIZE)
            right = weight[pl.ds(at, 2 * HEAD_SIZE), :]
            acc = acc + jnp.dot(left, right, preferred_element_type=jnp.float32)
        return acc

    acc = lax.fori_loop(
        0, QUERY_HEADS // 8, project, jnp.zeros((n, weight.shape[1]), jnp.float32)
    )
    panel[...] = acc.reshape(panel.shape)
    back = exchange(panel_column, sems.at[14], sems.at[15], segment, source=panel, in_plane=False)
    back[0]()
    panel_column[z] = panel[z]
    back[1]()
    for i in range(segment):
        for p in range(PROMPT_COUNT):
            panel_rows[i, p : p + 1, :] = panel_column[p, i : i + 1, :]
    home = exchange(out_ref, sems.at[16], sems.at[17], segment, source=panel_rows)
    home[0]()
    out_ref[j] = panel_rows[j]
    home[1]()
    for group in (ask, tell, tell_logs, answer_logs, share, share_logs, gather, back, home):
        group[2]()
    all_pairs(lambda i: ask_plane(i)[2]())
    all_pairs(lambda i: answer(i)[2]())


def body(
    queries,
    shared_prompt_keys,
    shared_prompt_values,
    private_cached_keys,
    private_cached_values,
    token_keys,
    token_values,
    suffix_lengths,
    block_prompts,
    out_weight,
):
    n = lax.axis_size("seq")
    segment = n // PROMPT_COUNT
    count, width = queries.shape
    assert count == 1 and block_prompts.shape[0] == PROMPT_COUNT
    heads, size = QUERY_HEADS, HEAD_SIZE
    columns = out_weight.shape[1]
    bf, f32 = jnp.bfloat16, jnp.float32
    most = max(segment, PROMPT_COUNT)
    own_keys, own_values = private_cached_keys[0], private_cached_values[0]
    out = pl.pallas_call(
        functools.partial(kernel, segment),
        out_shape=jax.ShapeDtypeStruct((segment, PROMPT_COUNT, columns), f32),
        in_specs=[SMEM, SMEM] + [VMEM] * 3 + [ANY] * 5,
        out_specs=VMEM,
        scratch_shapes=[
            pltpu.VMEM(own_keys.shape, bf),
            pltpu.VMEM(own_values.shape, bf),
            pltpu.VMEM(shared_prompt_keys.shape, bf),
            pltpu.VMEM(shared_prompt_values.shape, bf),
            pltpu.VMEM(out_weight.shape, bf),
            pltpu.VMEM((PROMPT_COUNT, heads, size), bf),
            pltpu.VMEM((segment, SLOTS, heads, size), bf),
            pltpu.VMEM((PROMPT_COUNT, heads, size), f32),
            pltpu.VMEM((PROMPT_COUNT, GROUP, 128), f32),
            pltpu.VMEM((segment, SLOTS, heads, size), bf),
            pltpu.VMEM((segment, SLOTS * GROUP, 128), f32),
            pltpu.VMEM((segment, SLOTS, heads, size), bf),
            pltpu.VMEM((segment, SLOTS * GROUP, 128), f32),
            pltpu.VMEM((PROMPT_COUNT, SLOTS, heads, size), bf),
            pltpu.VMEM((PROMPT_COUNT, SLOTS * GROUP, 128), f32),
            pltpu.VMEM((segment, PROMPT_COUNT, heads, size), bf),
            pltpu.VMEM((n * heads, size), f32),
            pltpu.VMEM((PROMPT_COUNT, segment, columns), f32),
            pltpu.VMEM((PROMPT_COUNT, segment, columns), f32),
            pltpu.VMEM((segment, PROMPT_COUNT, columns), f32),
            pltpu.SemaphoreType.DMA((5,)),
            pltpu.SemaphoreType.DMA((18, most)),
            pltpu.SemaphoreType.DMA((4, KEY_VALUE_HEADS // 2, most)),
        ],
        compiler_params=pltpu.CompilerParams(
            collective_id=0, has_side_effects=True, vmem_limit_bytes=56 << 20
        ),
    )(
        block_prompts,
        suffix_lengths,
        queries,
        token_keys,
        token_values,
        own_keys,
        own_values,
        shared_prompt_keys,
        shared_prompt_values,
        out_weight,
    )
    return out.transpose(1, 0, 2).reshape(1, width).astype(bf)


def solution(mesh):
    in_specs = (
        P(("groups", "seq"), None),
        P(("groups", "seq"), None),
        P(("groups", "seq"), None),
        P(("groups", "seq"), None, None),
        P(("groups", "seq"), None, None),
        P(("groups", "seq"), None),
        P(("groups", "seq"), None),
        P(("groups", "seq")),
        P("groups"),
        P(None, "seq"),
    )
    out_specs = P(("groups", "seq"), None)
    return jax.shard_map(body, mesh=mesh, in_specs=in_specs, out_specs=out_specs, check_vma=False)
```

```python
import functools
import math

import jax
import jax.numpy as jnp
from jax import lax
from jax.experimental import pallas as pl
from jax.experimental.pallas import tpu as pltpu
from jax.sharding import PartitionSpec as P

QUERY_HEADS = 64
KEY_VALUE_HEADS = 8
GROUP = QUERY_HEADS // KEY_VALUE_HEADS
HEAD_SIZE = 128
PROMPT_COUNT = 4
SLOTS = 2
SCALE = 1.0 / math.sqrt(HEAD_SIZE)
SCALE_LOG2 = SCALE * math.log2(math.e)
VMEM = pl.BlockSpec(memory_space=pltpu.VMEM)
ANY = pl.BlockSpec(memory_space=pl.ANY)
SMEM = pl.BlockSpec(memory_space=pltpu.SMEM)
NT = (((1,), (1,)), ((), ()))


def place(segment):
    me = lax.axis_index("seq")
    return me // segment, lax.rem(me, segment)


def each(count, step):
    if count <= 32:
        for d in range(1, count):
            step(d)
        return

    def one(i, carry):
        step(i + 1)
        return carry

    lax.fori_loop(0, count - 1, one, 0)


def greet(n):
    me = lax.axis_index("seq")
    sem = pltpu.get_barrier_semaphore()
    each(n, lambda d: pl.semaphore_signal(sem, inc=1, device_id={"seq": lax.rem(me + d, n)}))


def greeted(n):
    pl.semaphore_wait(pltpu.get_barrier_semaphore(), n - 1)


def exchange(ref, sems, segment, source=None, over="plane", rows=None):
    z, j = place(segment)
    n = segment * PROMPT_COUNT
    count, mine = {
        "plane": (segment, j),
        "column": (PROMPT_COUNT, z),
        "all": (n, lax.axis_index("seq")),
    }[over]
    send, recv = sems.at[0], sems.at[1]

    def view(array, block):
        return array.at[block] if rows is None else array.at[block, :, rows]

    def start():
        def copy(d):
            peer = lax.rem(mine + d, count)
            to = {"plane": z * segment + peer, "column": peer * segment + j, "all": peer}[over]
            pltpu.make_async_remote_copy(
                src_ref=view(ref, mine) if source is None else view(source, peer),
                dst_ref=view(ref, mine),
                send_sem=send,
                recv_sem=recv,
                device_id={"seq": to},
            ).start()

        each(count, copy)

    def wait(sem):
        whole = view(ref, pl.ds(0, count - 1))
        pltpu.make_async_copy(whole, whole, sem).wait()

    return start, lambda: wait(recv), lambda: wait(send)


def lanes(shape):
    return lax.broadcasted_iota(jnp.int32, shape, len(shape) - 1)


def pick(at, choices):
    at = jnp.full(choices[0].shape, at, jnp.int32)
    out = choices[0]
    for i, choice in enumerate(choices[1:]):
        out = jnp.where(at == i + 1, choice, out)
    return out


def own_suffix(heads, logs, length, q, keys_ref, values_ref, key_ref, value_ref):
    parts = []
    slots = keys_ref.shape[0]
    live = lanes((GROUP, slots)) < length
    for k in heads:
        cut = slice(k * HEAD_SIZE, (k + 1) * HEAD_SIZE)
        head = q[k * GROUP : (k + 1) * GROUP]
        scores = lax.dot_general(
            head.astype(jnp.bfloat16), keys_ref[:, cut], NT, preferred_element_type=jnp.float32
        )
        scores = jnp.where(live, scores * SCALE, -1e30)
        fresh = jnp.sum(head * key_ref[:, cut].astype(jnp.float32), axis=1, keepdims=True) * SCALE
        top = jnp.maximum(jnp.max(scores, axis=1, keepdims=True), fresh)
        weights = jnp.exp(scores - top)
        fresh_weight = jnp.exp(fresh - top)
        total = jnp.sum(weights, axis=1, keepdims=True) + fresh_weight
        out = jnp.dot(
            weights.astype(jnp.bfloat16), values_ref[:, cut], preferred_element_type=jnp.float32
        )
        fresh_weight = fresh_weight.astype(jnp.bfloat16).astype(jnp.float32)
        out = out + fresh_weight * value_ref[:, cut].astype(jnp.float32)
        parts.append(out / total)
        logs = jnp.where(lanes(logs.shape) == k, top + jnp.log(total), logs)
    return jnp.concatenate(parts, axis=0), logs


def spread(weights, pair):
    first = weights[:, 2 * pair : 2 * pair + 1]
    second = weights[:, 2 * pair + 1 : 2 * pair + 2]
    return jnp.concatenate([first, second], axis=0)


def pair_rows(i):
    return pl.ds(pl.multiple_of(i * 16, 16), 16)


def attend(i, segment, q_ref, keys_ref, values_ref, part_ref, logs_ref):
    rows = segment * SLOTS * GROUP
    q = q_ref[:, :, pair_rows(i), :].astype(jnp.float32)
    q = q.reshape(segment * SLOTS, 2, GROUP, HEAD_SIZE)
    parts = []
    logs = logs_ref[...].reshape(rows, 128)
    for h in range(2):
        cut = pl.ds(pl.multiple_of((i * 2 + h) * HEAD_SIZE, HEAD_SIZE), HEAD_SIZE)
        head = q[:, h].reshape(rows, HEAD_SIZE).astype(jnp.bfloat16)
        scores = lax.dot_general(head, keys_ref[:, cut], NT, preferred_element_type=jnp.float32)
        top = jnp.max(scores, axis=1, keepdims=True)
        weights = jnp.exp2((scores - top) * SCALE_LOG2)
        total = jnp.sum(weights, axis=1, keepdims=True)
        out = jnp.dot(
            weights.astype(jnp.bfloat16), values_ref[:, cut], preferred_element_type=jnp.float32
        )
        parts.append((out / total).reshape(segment * SLOTS, GROUP, HEAD_SIZE))
        logs = jnp.where(lanes(logs.shape) == i * 2 + h, top * SCALE + jnp.log(total), logs)
    logs_ref[...] = logs.reshape(logs_ref.shape)
    both = jnp.concatenate(parts, axis=1).astype(jnp.bfloat16)
    part_ref[:, :, pair_rows(i), :] = both.reshape(segment, SLOTS, 16, HEAD_SIZE)


def kernel(
    segment,
    prompts_ref,
    length_ref,
    q_ref,
    key_ref,
    value_ref,
    own_keys_hbm,
    own_values_hbm,
    keys_hbm,
    values_hbm,
    weight_hbm,
    out_ref,
    own_keys,
    own_values,
    keys,
    values,
    weight,
    q_column,
    q_all,
    suffix,
    suffix_logs,
    parts,
    logs,
    got,
    got_logs,
    column,
    column_logs,
    rows_all,
    rows_wide,
    panel,
    local_sems,
    sems,
    chunk_sems,
):
    z, j = place(segment)
    n = segment * PROMPT_COUNT
    greet(n)
    loads = [
        pltpu.make_async_copy(src, dst, local_sems.at[i])
        for i, (src, dst) in enumerate(
            (
                (own_keys_hbm, own_keys),
                (own_values_hbm, own_values),
                (keys_hbm, keys),
                (values_hbm, values),
                (weight_hbm, weight),
            )
        )
    ]
    for load in loads:
        load.start()

    flat = q_ref[...].astype(jnp.float32)
    q = jnp.concatenate(
        [flat[:, h * HEAD_SIZE : (h + 1) * HEAD_SIZE] for h in range(QUERY_HEADS)], axis=0
    )
    q_column[z] = q.astype(jnp.bfloat16)
    logs[...] = jnp.zeros_like(logs)
    prompts = [prompts_ref[b] for b in range(PROMPT_COUNT)]
    ranks = []
    for b in range(PROMPT_COUNT):
        rank = jnp.int32(0)
        for c in range(b):
            rank = rank + jnp.where(prompts[c] == prompts[b], 1, 0)
        ranks.append(rank)
    slot_block = []
    for s in range(SLOTS):
        block = jnp.int32(0)
        for b in range(PROMPT_COUNT):
            block = jnp.where((prompts[b] == z) & (ranks[b] == s), b, block)
        slot_block.append(block)

    greeted(n)
    ask = exchange(q_column, sems.at[0], segment, over="column")
    ask[0]()
    loads[0].wait()
    loads[1].wait()
    halves = []
    own_logs = jnp.zeros((GROUP, 128), jnp.float32)
    own = (length_ref[0], q, own_keys, own_values, key_ref, value_ref)
    half, own_logs = own_suffix(range(4), own_logs, *own)
    halves.append(half)
    ask[1]()
    for s in range(SLOTS):
        q_all[j, s] = pick(slot_block[s], [q_column[b] for b in range(PROMPT_COUNT)])

    def ask_plane(i):
        return exchange(q_all, chunk_sems.at[0, i], segment, rows=pair_rows(i))

    def answer(i):
        return exchange(got, chunk_sems.at[1, i], segment, source=parts, rows=pair_rows(i))

    pairs = KEY_VALUE_HEADS // 2

    def all_pairs(step):
        def one(i, carry):
            step(i)
            return carry

        lax.fori_loop(0, pairs, one, 0)

    all_pairs(lambda i: ask_plane(i)[0]())
    half, own_logs = own_suffix(range(4, KEY_VALUE_HEADS), own_logs, *own)
    halves.append(half)
    suffix[z] = jnp.concatenate(halves, axis=0)
    suffix_logs[z] = own_logs
    tell = exchange(suffix, sems.at[1], segment, over="column")
    tell_logs = exchange(suffix_logs, sems.at[2], segment, over="column")
    tell[0]()
    tell_logs[0]()
    loads[2].wait()
    loads[3].wait()

    def work(i):
        ask_plane(i)[1]()
        attend(i, segment, q_all, keys, values, parts, logs)
        answer(i)[0]()

    all_pairs(work)
    answer_logs = exchange(got_logs, sems.at[3], segment, source=logs)
    answer_logs[0]()
    got[j] = parts[j]
    got_logs[j] = logs[j]
    answer_logs[1]()
    all_logs = got_logs[...]
    best = jnp.max(all_logs, axis=0)
    weights = jnp.exp(all_logs - best[None])
    total = jnp.sum(weights, axis=0)
    weights = weights / total[None]
    column_logs[z] = best + jnp.log(total)
    all_pairs(lambda i: answer(i)[1]())
    for s in range(SLOTS):
        for pair in range(pairs):
            rows = slice(pair * 16, pair * 16 + 16)
            acc = jnp.zeros((16, HEAD_SIZE), jnp.float32)
            for i in range(segment):
                w = spread(weights[i, s * GROUP : (s + 1) * GROUP], pair)
                acc = acc + w * got[i, s, rows].astype(jnp.float32)
            column[z, s, rows] = acc.astype(jnp.bfloat16)
    share = exchange(column, sems.at[4], segment, over="column")
    share_logs = exchange(column_logs, sems.at[5], segment, over="column")
    share_logs[0]()
    share[0]()
    tell_logs[1]()
    tell[1]()
    share_logs[1]()
    share[1]()
    for b in range(PROMPT_COUNT):
        at = prompts[b] * SLOTS + ranks[b]
        prompt = pick(at, [column[i // SLOTS, i % SLOTS] for i in range(PROMPT_COUNT * SLOTS)])
        prompt = prompt.astype(jnp.float32)
        prompt_logs = pick(
            at,
            [
                column_logs[p, s * GROUP : (s + 1) * GROUP]
                for p in range(PROMPT_COUNT)
                for s in range(SLOTS)
            ],
        )
        own_logs = suffix_logs[b]
        best = jnp.maximum(prompt_logs, own_logs)
        prompt_weight = jnp.exp(prompt_logs - best)
        own_weight = jnp.exp(own_logs - best)
        total = prompt_weight + own_weight
        prompt_weight = prompt_weight / total
        own_weight = own_weight / total
        for pair in range(pairs):
            rows = slice(pair * 16, pair * 16 + 16)
            row = spread(prompt_weight, pair) * prompt[rows]
            row = row + spread(own_weight, pair) * suffix[b, rows]
            rows_all[j, b, rows] = row.astype(jnp.bfloat16)
    gather = exchange(rows_all, sems.at[6], segment)
    gather[0]()
    loads[4].wait()
    for group in (ask, tell, tell_logs, answer_logs, share, share_logs):
        group[2]()
    all_pairs(lambda i: ask_plane(i)[2]())
    all_pairs(lambda i: answer(i)[2]())
    gather[1]()

    def widen(i, carry):
        for b in range(PROMPT_COUNT):
            at = pl.multiple_of((b * segment + i) * QUERY_HEADS, QUERY_HEADS)
            rows_wide[pl.ds(at, QUERY_HEADS), :] = rows_all[i, b].astype(jnp.float32)
        return carry

    lax.fori_loop(0, segment, widen, 0)

    def project(i, acc):
        for pair in range(4):
            h = i * 8 + pair * 2
            both = [rows_wide[pl.ds(h + o, n, stride=QUERY_HEADS), :] for o in range(2)]
            left = jnp.concatenate(both, axis=1).astype(jnp.bfloat16)
            at = pl.multiple_of(h * HEAD_SIZE, 2 * HEAD_SIZE)
            right = weight[pl.ds(at, 2 * HEAD_SIZE), :]
            acc = acc + jnp.dot(left, right, preferred_element_type=jnp.float32)
        return acc

    acc = lax.fori_loop(
        0, QUERY_HEADS // 8, project, jnp.zeros((n, weight.shape[1]), jnp.float32)
    )
    for r in range(n):
        panel[r] = acc[r : r + 1]
    home = exchange(out_ref, sems.at[7], segment, source=panel, over="all")
    home[0]()
    me = lax.axis_index("seq")
    out_ref[me] = panel[me]
    gather[2]()
    home[1]()
    home[2]()


def body(
    queries,
    shared_prompt_keys,
    shared_prompt_values,
    private_cached_keys,
    private_cached_values,
    token_keys,
    token_values,
    suffix_lengths,
    block_prompts,
    out_weight,
):
    n = lax.axis_size("seq")
    segment = n // PROMPT_COUNT
    count, width = queries.shape
    assert count == 1 and block_prompts.shape[0] == PROMPT_COUNT
    heads, size = QUERY_HEADS, HEAD_SIZE
    columns = out_weight.shape[1]
    bf, f32 = jnp.bfloat16, jnp.float32
    own_keys, own_values = private_cached_keys[0], private_cached_values[0]
    out = pl.pallas_call(
        functools.partial(kernel, segment),
        out_shape=jax.ShapeDtypeStruct((n, 1, columns), f32),
        in_specs=[SMEM, SMEM] + [VMEM] * 3 + [ANY] * 5,
        out_specs=VMEM,
        scratch_shapes=[
            pltpu.VMEM(own_keys.shape, bf),
            pltpu.VMEM(own_values.shape, bf),
            pltpu.VMEM(shared_prompt_keys.shape, bf),
            pltpu.VMEM(shared_prompt_values.shape, bf),
            pltpu.VMEM(out_weight.shape, bf),
            pltpu.VMEM((PROMPT_COUNT, heads, size), bf),
            pltpu.VMEM((segment, SLOTS, heads, size), bf),
            pltpu.VMEM((PROMPT_COUNT, heads, size), f32),
            pltpu.VMEM((PROMPT_COUNT, GROUP, 128), f32),
            pltpu.VMEM((segment, SLOTS, heads, size), bf),
            pltpu.VMEM((segment, SLOTS * GROUP, 128), f32),
            pltpu.VMEM((segment, SLOTS, heads, size), bf),
            pltpu.VMEM((segment, SLOTS * GROUP, 128), f32),
            pltpu.VMEM((PROMPT_COUNT, SLOTS, heads, size), bf),
            pltpu.VMEM((PROMPT_COUNT, SLOTS * GROUP, 128), f32),
            pltpu.VMEM((segment, PROMPT_COUNT, heads, size), bf),
            pltpu.VMEM((n * heads, size), f32),
            pltpu.VMEM((n, 1, columns), f32),
            pltpu.SemaphoreType.DMA((5,)),
            pltpu.SemaphoreType.DMA((8, 2)),
            pltpu.SemaphoreType.DMA((2, KEY_VALUE_HEADS // 2, 2)),
        ],
        compiler_params=pltpu.CompilerParams(
            collective_id=0, has_side_effects=True, vmem_limit_bytes=56 << 20
        ),
    )(
        block_prompts,
        suffix_lengths,
        queries,
        token_keys,
        token_values,
        own_keys,
        own_values,
        shared_prompt_keys,
        shared_prompt_values,
        out_weight,
    )
    return out.reshape(1, width).astype(bf)


def solution(mesh):
    in_specs = (
        P(("groups", "seq"), None),
        P(("groups", "seq"), None),
        P(("groups", "seq"), None),
        P(("groups", "seq"), None, None),
        P(("groups", "seq"), None, None),
        P(("groups", "seq"), None),
        P(("groups", "seq"), None),
        P(("groups", "seq")),
        P("groups"),
        P(None, "seq"),
    )
    out_specs = P(("groups", "seq"), None)
    return jax.shard_map(body, mesh=mesh, in_specs=in_specs, out_specs=out_specs, check_vma=False)
```

```python
import functools
import math

import jax
import jax.numpy as jnp
from jax import lax
from jax.experimental import pallas as pl
from jax.experimental.pallas import tpu as pltpu
from jax.sharding import PartitionSpec as P

QUERY_HEADS = 64
KEY_VALUE_HEADS = 8
GROUP = QUERY_HEADS // KEY_VALUE_HEADS
HEAD_SIZE = 128
PROMPT_COUNT = 4
SLOTS = 2
HALF_HEADS = QUERY_HEADS // 2
SCALE = 1.0 / math.sqrt(HEAD_SIZE)
SCALE_LOG2 = SCALE * math.log2(math.e)
VMEM = pl.BlockSpec(memory_space=pltpu.VMEM)
ANY = pl.BlockSpec(memory_space=pl.ANY)
SMEM = pl.BlockSpec(memory_space=pltpu.SMEM)
NT = (((1,), (1,)), ((), ()))


def place(segment):
    me = lax.axis_index("seq")
    return me // segment, lax.rem(me, segment)


def each(count, step):
    if count <= 32:
        for d in range(1, count):
            step(d)
        return

    def one(i, carry):
        step(i + 1)
        return carry

    lax.fori_loop(0, count - 1, one, 0)


def greet(n):
    me = lax.axis_index("seq")
    sem = pltpu.get_barrier_semaphore()
    each(n, lambda d: pl.semaphore_signal(sem, inc=1, device_id={"seq": lax.rem(me + d, n)}))


def greeted(n):
    pl.semaphore_wait(pltpu.get_barrier_semaphore(), n - 1)


def exchange(ref, sems, segment, source=None, over="plane", rows=None):
    z, j = place(segment)
    n = segment * PROMPT_COUNT
    count, mine = {
        "plane": (segment, j),
        "column": (PROMPT_COUNT, z),
        "all": (n, lax.axis_index("seq")),
    }[over]
    send, recv = sems.at[0], sems.at[1]

    def view(array, block):
        return array.at[block] if rows is None else array.at[block, :, rows]

    def start():
        def copy(d):
            peer = lax.rem(mine + d, count)
            to = {"plane": z * segment + peer, "column": peer * segment + j, "all": peer}[over]
            pltpu.make_async_remote_copy(
                src_ref=view(ref, mine) if source is None else view(source, peer),
                dst_ref=view(ref, mine),
                send_sem=send,
                recv_sem=recv,
                device_id={"seq": to},
            ).start()

        each(count, copy)

    def wait(sem):
        whole = view(ref, pl.ds(0, count - 1))
        pltpu.make_async_copy(whole, whole, sem).wait()

    return start, lambda: wait(recv), lambda: wait(send)


def lanes(shape):
    return lax.broadcasted_iota(jnp.int32, shape, len(shape) - 1)


def pick(at, choices):
    at = jnp.full(choices[0].shape, at, jnp.int32)
    out = choices[0]
    for i, choice in enumerate(choices[1:]):
        out = jnp.where(at == i + 1, choice, out)
    return out


def own_suffix(heads, logs, length, q, keys_ref, values_ref, key_ref, value_ref):
    parts = []
    slots = keys_ref.shape[0]
    live = lanes((GROUP, slots)) < length
    for k in heads:
        cut = slice(k * HEAD_SIZE, (k + 1) * HEAD_SIZE)
        head = q[k * GROUP : (k + 1) * GROUP]
        scores = lax.dot_general(
            head.astype(jnp.bfloat16), keys_ref[:, cut], NT, preferred_element_type=jnp.float32
        )
        scores = jnp.where(live, scores * SCALE, -1e30)
        fresh = jnp.sum(head * key_ref[:, cut].astype(jnp.float32), axis=1, keepdims=True) * SCALE
        top = jnp.maximum(jnp.max(scores, axis=1, keepdims=True), fresh)
        weights = jnp.exp(scores - top)
        fresh_weight = jnp.exp(fresh - top)
        total = jnp.sum(weights, axis=1, keepdims=True) + fresh_weight
        out = jnp.dot(
            weights.astype(jnp.bfloat16), values_ref[:, cut], preferred_element_type=jnp.float32
        )
        fresh_weight = fresh_weight.astype(jnp.bfloat16).astype(jnp.float32)
        out = out + fresh_weight * value_ref[:, cut].astype(jnp.float32)
        parts.append(out / total)
        logs = jnp.where(lanes(logs.shape) == k, top + jnp.log(total), logs)
    return jnp.concatenate(parts, axis=0), logs


def spread(weights, pair):
    first = weights[:, 2 * pair : 2 * pair + 1]
    second = weights[:, 2 * pair + 1 : 2 * pair + 2]
    return jnp.concatenate([first, second], axis=0)


def pair_rows(i):
    return pl.ds(i * 16, 16)


def attend(i, segment, q_ref, keys_ref, values_ref, part_ref, logs_ref):
    rows = segment * SLOTS * GROUP
    q = q_ref[:, :, pair_rows(i), :].astype(jnp.float32)
    q = q.reshape(segment * SLOTS, 2, GROUP, HEAD_SIZE)
    parts = []
    logs = logs_ref[...].reshape(rows, 128)
    for h in range(2):
        cut = pl.ds((i * 2 + h) * HEAD_SIZE, HEAD_SIZE)
        head = q[:, h].reshape(rows, HEAD_SIZE).astype(jnp.bfloat16)
        scores = lax.dot_general(head, keys_ref[:, cut], NT, preferred_element_type=jnp.float32)
        top = jnp.max(scores, axis=1, keepdims=True)
        weights = jnp.exp2((scores - top) * SCALE_LOG2)
        total = jnp.sum(weights, axis=1, keepdims=True)
        out = jnp.dot(
            weights.astype(jnp.bfloat16), values_ref[:, cut], preferred_element_type=jnp.float32
        )
        parts.append((out / total).reshape(segment * SLOTS, GROUP, HEAD_SIZE))
        logs = jnp.where(lanes(logs.shape) == i * 2 + h, top * SCALE + jnp.log(total), logs)
    logs_ref[...] = logs.reshape(logs_ref.shape)
    both = jnp.concatenate(parts, axis=1).astype(jnp.bfloat16)
    part_ref[:, :, pair_rows(i), :] = both.reshape(segment, SLOTS, 16, HEAD_SIZE)


def kernel(
    segment,
    prompts_ref,
    length_ref,
    q_ref,
    key_ref,
    value_ref,
    own_keys_hbm,
    own_values_hbm,
    keys_hbm,
    values_hbm,
    weight_hbm,
    out_ref,
    own_keys,
    own_values,
    keys,
    values,
    weight,
    q_column,
    q_all,
    suffix,
    suffix_logs,
    parts,
    logs,
    got,
    got_logs,
    column,
    column_logs,
    rows_all,
    rows_wide,
    panel,
    local_sems,
    sems,
    chunk_sems,
):
    z, j = place(segment)
    n = segment * PROMPT_COUNT
    greet(n)
    loads = [
        pltpu.make_async_copy(src, dst, local_sems.at[i])
        for i, (src, dst) in enumerate(
            (
                (own_keys_hbm, own_keys),
                (own_values_hbm, own_values),
                (keys_hbm, keys),
                (values_hbm, values),
                (weight_hbm, weight),
            )
        )
    ]
    for load in loads:
        load.start()

    flat = q_ref[...].astype(jnp.float32)
    q = jnp.concatenate(
        [flat[:, h * HEAD_SIZE : (h + 1) * HEAD_SIZE] for h in range(QUERY_HEADS)], axis=0
    )
    q_column[z] = q.astype(jnp.bfloat16)
    logs[...] = jnp.zeros_like(logs)
    prompts = [prompts_ref[b] for b in range(PROMPT_COUNT)]
    ranks = []
    for b in range(PROMPT_COUNT):
        rank = jnp.int32(0)
        for c in range(b):
            rank = rank + jnp.where(prompts[c] == prompts[b], 1, 0)
        ranks.append(rank)
    slot_block = []
    for s in range(SLOTS):
        block = jnp.int32(0)
        for b in range(PROMPT_COUNT):
            block = jnp.where((prompts[b] == z) & (ranks[b] == s), b, block)
        slot_block.append(block)

    greeted(n)
    ask = exchange(q_column, sems.at[0], segment, over="column")
    ask[0]()
    loads[0].wait()
    loads[1].wait()
    halves = []
    own_logs = jnp.zeros((GROUP, 128), jnp.float32)
    own = (length_ref[0], q, own_keys, own_values, key_ref, value_ref)
    part, own_logs = own_suffix(range(4), own_logs, *own)
    halves.append(part)
    ask[1]()
    for s in range(SLOTS):
        q_all[j, s] = pick(slot_block[s], [q_column[b] for b in range(PROMPT_COUNT)])

    def ask_plane(i):
        return exchange(q_all, chunk_sems.at[0, i], segment, rows=pair_rows(i))

    def answer(i):
        return exchange(got, chunk_sems.at[1, i], segment, source=parts, rows=pair_rows(i))

    pairs = KEY_VALUE_HEADS // 2
    half = pairs // 2

    def head_rows(c):
        return pl.ds(c * HALF_HEADS, HALF_HEADS)

    def answer_logs(c):
        return exchange(got_logs.at[c], sems.at[3 + c], segment, source=logs.at[c])

    def share(c):
        return exchange(column, sems.at[5 + c], segment, over="column", rows=head_rows(c))

    def share_logs(c):
        return exchange(column_logs.at[c], sems.at[7 + c], segment, over="column")

    def gather(c):
        return exchange(rows_all, sems.at[9 + c], segment, rows=head_rows(c))

    for i in range(pairs):
        ask_plane(i)[0]()
    part, own_logs = own_suffix(range(4, KEY_VALUE_HEADS), own_logs, *own)
    halves.append(part)
    suffix[z] = jnp.concatenate(halves, axis=0)
    suffix_logs[z] = own_logs
    tell = exchange(suffix, sems.at[1], segment, over="column")
    tell_logs = exchange(suffix_logs, sems.at[2], segment, over="column")
    tell[0]()
    tell_logs[0]()
    loads[2].wait()
    loads[3].wait()

    def work(i):
        c = i // half
        ask_plane(i)[1]()
        attend(i, segment, q_all, keys, values, parts, logs.at[c])
        answer(i)[0]()
        if i % half == half - 1:
            answer_logs(c)[0]()
            got_logs[c, j] = logs[c, j]
        got[j, :, pair_rows(i), :] = parts[j, :, pair_rows(i), :]

    def combine(c):
        answer_logs(c)[1]()
        all_logs = got_logs[c]
        best = jnp.max(all_logs, axis=0)
        weights = jnp.exp(all_logs - best[None])
        total = jnp.sum(weights, axis=0)
        weights = weights / total[None]
        column_logs[c, z] = best + jnp.log(total)
        share_logs(c)[0]()
        for pair in range(c * half, (c + 1) * half):
            answer(pair)[1]()
            for s in range(SLOTS):
                rows = slice(pair * 16, pair * 16 + 16)
                acc = jnp.zeros((16, HEAD_SIZE), jnp.float32)
                for i in range(segment):
                    w = spread(weights[i, s * GROUP : (s + 1) * GROUP], pair)
                    acc = acc + w * got[i, s, rows].astype(jnp.float32)
                column[z, s, rows] = acc.astype(jnp.bfloat16)
        share(c)[0]()

    def finish_rows(c):
        share_logs(c)[1]()
        share(c)[1]()
        for b in range(PROMPT_COUNT):
            at = prompts[b] * SLOTS + ranks[b]
            prompt_logs = pick(
                at,
                [
                    column_logs[c, p, s * GROUP : (s + 1) * GROUP]
                    for p in range(PROMPT_COUNT)
                    for s in range(SLOTS)
                ],
            )
            own_logs = suffix_logs[b]
            best = jnp.maximum(prompt_logs, own_logs)
            prompt_weight = jnp.exp(prompt_logs - best)
            own_weight = jnp.exp(own_logs - best)
            total = prompt_weight + own_weight
            prompt_weight = prompt_weight / total
            own_weight = own_weight / total
            for pair in range(c * half, (c + 1) * half):
                rows = slice(pair * 16, pair * 16 + 16)
                prompt = pick(
                    at, [column[i // SLOTS, i % SLOTS, rows] for i in range(PROMPT_COUNT * SLOTS)]
                )
                row = spread(prompt_weight, pair) * prompt.astype(jnp.float32)
                row = row + spread(own_weight, pair) * suffix[b, rows]
                rows_all[j, b, rows] = row.astype(jnp.bfloat16)
        gather(c)[0]()

    def project(c, acc):
        gather(c)[1]()

        def widen(i, carry):
            for b in range(PROMPT_COUNT):
                at = (b * segment + i) * QUERY_HEADS + c * HALF_HEADS
                rows_wide[pl.ds(pl.multiple_of(at, HALF_HEADS), HALF_HEADS), :] = rows_all[
                    i, b, head_rows(c), :
                ].astype(jnp.float32)
            return carry

        lax.fori_loop(0, segment, widen, 0)

        def some(i, acc):
            for pair in range(4):
                h = i * 8 + pair * 2
                both = [rows_wide[pl.ds(h + o, n, stride=QUERY_HEADS), :] for o in range(2)]
                left = jnp.concatenate(both, axis=1).astype(jnp.bfloat16)
                at = pl.multiple_of(h * HEAD_SIZE, 2 * HEAD_SIZE)
                right = weight[pl.ds(at, 2 * HEAD_SIZE), :]
                acc = acc + jnp.dot(left, right, preferred_element_type=jnp.float32)
            return acc

        return lax.fori_loop(c * HALF_HEADS // 8, (c + 1) * HALF_HEADS // 8, some, acc)

    work(0)
    work(1)
    work(2)
    combine(0)
    work(3)
    tell_logs[1]()
    tell[1]()
    finish_rows(0)
    combine(1)
    loads[4].wait()
    for group in (ask, tell, tell_logs, answer_logs(0), answer_logs(1), share_logs(0), share(0)):
        group[2]()
    for i in range(pairs):
        ask_plane(i)[2]()
        answer(i)[2]()
    acc = project(0, jnp.zeros((n, weight.shape[1]), jnp.float32))
    finish_rows(1)
    share_logs(1)[2]()
    share(1)[2]()
    acc = project(1, acc)
    for r in range(n):
        panel[r] = acc[r : r + 1]
    home = exchange(out_ref, sems.at[11], segment, source=panel, over="all")
    home[0]()
    me = lax.axis_index("seq")
    out_ref[me] = panel[me]
    gather(0)[2]()
    gather(1)[2]()
    home[1]()
    home[2]()


def body(
    queries,
    shared_prompt_keys,
    shared_prompt_values,
    private_cached_keys,
    private_cached_values,
    token_keys,
    token_values,
    suffix_lengths,
    block_prompts,
    out_weight,
):
    n = lax.axis_size("seq")
    segment = n // PROMPT_COUNT
    count, width = queries.shape
    assert count == 1 and block_prompts.shape[0] == PROMPT_COUNT
    heads, size = QUERY_HEADS, HEAD_SIZE
    columns = out_weight.shape[1]
    bf, f32 = jnp.bfloat16, jnp.float32
    own_keys, own_values = private_cached_keys[0], private_cached_values[0]
    out = pl.pallas_call(
        functools.partial(kernel, segment),
        out_shape=jax.ShapeDtypeStruct((n, 1, columns), f32),
        in_specs=[SMEM, SMEM] + [VMEM] * 3 + [ANY] * 5,
        out_specs=VMEM,
        scratch_shapes=[
            pltpu.VMEM(own_keys.shape, bf),
            pltpu.VMEM(own_values.shape, bf),
            pltpu.VMEM(shared_prompt_keys.shape, bf),
            pltpu.VMEM(shared_prompt_values.shape, bf),
            pltpu.VMEM(out_weight.shape, bf),
            pltpu.VMEM((PROMPT_COUNT, heads, size), bf),
            pltpu.VMEM((segment, SLOTS, heads, size), bf),
            pltpu.VMEM((PROMPT_COUNT, heads, size), f32),
            pltpu.VMEM((PROMPT_COUNT, GROUP, 128), f32),
            pltpu.VMEM((segment, SLOTS, heads, size), bf),
            pltpu.VMEM((2, segment, SLOTS * GROUP, 128), f32),
            pltpu.VMEM((segment, SLOTS, heads, size), bf),
            pltpu.VMEM((2, segment, SLOTS * GROUP, 128), f32),
            pltpu.VMEM((PROMPT_COUNT, SLOTS, heads, size), bf),
            pltpu.VMEM((2, PROMPT_COUNT, SLOTS * GROUP, 128), f32),
            pltpu.VMEM((segment, PROMPT_COUNT, heads, size), bf),
            pltpu.VMEM((n * heads, size), f32),
            pltpu.VMEM((n, 1, columns), f32),
            pltpu.SemaphoreType.DMA((5,)),
            pltpu.SemaphoreType.DMA((12, 2)),
            pltpu.SemaphoreType.DMA((2, KEY_VALUE_HEADS // 2, 2)),
        ],
        compiler_params=pltpu.CompilerParams(
            collective_id=0, has_side_effects=True, vmem_limit_bytes=56 << 20
        ),
    )(
        block_prompts,
        suffix_lengths,
        queries,
        token_keys,
        token_values,
        own_keys,
        own_values,
        shared_prompt_keys,
        shared_prompt_values,
        out_weight,
    )
    return out.reshape(1, width).astype(bf)


def solution(mesh):
    in_specs = (
        P(("groups", "seq"), None),
        P(("groups", "seq"), None),
        P(("groups", "seq"), None),
        P(("groups", "seq"), None, None),
        P(("groups", "seq"), None, None),
        P(("groups", "seq"), None),
        P(("groups", "seq"), None),
        P(("groups", "seq")),
        P("groups"),
        P(None, "seq"),
    )
    out_specs = P(("groups", "seq"), None)
    return jax.shard_map(body, mesh=mesh, in_specs=in_specs, out_specs=out_specs, check_vma=False)
```

```python
import functools
import math

import jax
import jax.numpy as jnp
from jax import lax
from jax.experimental import pallas as pl
from jax.experimental.pallas import tpu as pltpu
from jax.sharding import PartitionSpec as P

QUERY_HEADS = 64
KEY_VALUE_HEADS = 8
GROUP = QUERY_HEADS // KEY_VALUE_HEADS
HEAD_SIZE = 128
PROMPT_COUNT = 4
SLOTS = 2
HALF_HEADS = QUERY_HEADS // 2
SCALE = 1.0 / math.sqrt(HEAD_SIZE)
SCALE_LOG2 = SCALE * math.log2(math.e)
VMEM = pl.BlockSpec(memory_space=pltpu.VMEM)
ANY = pl.BlockSpec(memory_space=pl.ANY)
SMEM = pl.BlockSpec(memory_space=pltpu.SMEM)
NT = (((1,), (1,)), ((), ()))


def place(segment):
    me = lax.axis_index("seq")
    return me // segment, lax.rem(me, segment)


def each(count, step):
    if count <= 32:
        for d in range(1, count):
            step(d)
        return

    def one(i, carry):
        step(i + 1)
        return carry

    lax.fori_loop(0, count - 1, one, 0)


def greet(n):
    me = lax.axis_index("seq")
    sem = pltpu.get_barrier_semaphore()
    each(n, lambda d: pl.semaphore_signal(sem, inc=1, device_id={"seq": lax.rem(me + d, n)}))


def greeted(n):
    pl.semaphore_wait(pltpu.get_barrier_semaphore(), n - 1)


def exchange(ref, sems, segment, source=None, over="plane", rows=None):
    z, j = place(segment)
    n = segment * PROMPT_COUNT
    count, mine = {
        "plane": (segment, j),
        "column": (PROMPT_COUNT, z),
        "all": (n, lax.axis_index("seq")),
    }[over]
    send, recv = sems.at[0], sems.at[1]

    def view(array, block):
        return array.at[block] if rows is None else array.at[block, :, rows]

    def start():
        def copy(d):
            peer = lax.rem(mine + d, count)
            to = {"plane": z * segment + peer, "column": peer * segment + j, "all": peer}[over]
            pltpu.make_async_remote_copy(
                src_ref=view(ref, mine) if source is None else view(source, peer),
                dst_ref=view(ref, mine),
                send_sem=send,
                recv_sem=recv,
                device_id={"seq": to},
            ).start()

        each(count, copy)

    def wait(sem):
        whole = view(ref, pl.ds(0, count - 1))
        pltpu.make_async_copy(whole, whole, sem).wait()

    return start, lambda: wait(recv), lambda: wait(send)


def lanes(shape):
    return lax.broadcasted_iota(jnp.int32, shape, len(shape) - 1)


def pick(at, choices):
    at = jnp.full(choices[0].shape, at, jnp.int32)
    out = choices[0]
    for i, choice in enumerate(choices[1:]):
        out = jnp.where(at == i + 1, choice, out)
    return out


def own_suffix(heads, logs, length, q, keys_ref, values_ref, key_ref, value_ref):
    parts = []
    slots = keys_ref.shape[0]
    live = lanes((GROUP, slots)) < length
    for k in heads:
        cut = slice(k * HEAD_SIZE, (k + 1) * HEAD_SIZE)
        head = q[k * GROUP : (k + 1) * GROUP]
        scores = lax.dot_general(
            head.astype(jnp.bfloat16), keys_ref[:, cut], NT, preferred_element_type=jnp.float32
        )
        scores = jnp.where(live, scores * SCALE, -1e30)
        fresh = jnp.sum(head * key_ref[:, cut].astype(jnp.float32), axis=1, keepdims=True) * SCALE
        top = jnp.maximum(jnp.max(scores, axis=1, keepdims=True), fresh)
        weights = jnp.exp(scores - top)
        fresh_weight = jnp.exp(fresh - top)
        total = jnp.sum(weights, axis=1, keepdims=True) + fresh_weight
        out = jnp.dot(
            weights.astype(jnp.bfloat16), values_ref[:, cut], preferred_element_type=jnp.float32
        )
        fresh_weight = fresh_weight.astype(jnp.bfloat16).astype(jnp.float32)
        out = out + fresh_weight * value_ref[:, cut].astype(jnp.float32)
        parts.append(out / total)
        logs = jnp.where(lanes(logs.shape) == k, top + jnp.log(total), logs)
    return jnp.concatenate(parts, axis=0), logs


def spread(weights, pair):
    first = weights[:, 2 * pair : 2 * pair + 1]
    second = weights[:, 2 * pair + 1 : 2 * pair + 2]
    return jnp.concatenate([first, second], axis=0)


def pair_rows(i):
    return pl.ds(i * 16, 16)


def attend(i, segment, q_ref, keys_ref, values_ref, part_ref, logs_ref):
    rows = segment * SLOTS * GROUP
    q = q_ref[:, :, pair_rows(i), :].astype(jnp.float32)
    q = q.reshape(segment * SLOTS, 2, GROUP, HEAD_SIZE)
    parts = []
    logs = logs_ref[...].reshape(rows, 128)
    for h in range(2):
        cut = pl.ds((i * 2 + h) * HEAD_SIZE, HEAD_SIZE)
        head = q[:, h].reshape(rows, HEAD_SIZE).astype(jnp.bfloat16)
        scores = lax.dot_general(head, keys_ref[:, cut], NT, preferred_element_type=jnp.float32)
        top = jnp.max(scores, axis=1, keepdims=True)
        weights = jnp.exp2((scores - top) * SCALE_LOG2)
        total = jnp.sum(weights, axis=1, keepdims=True)
        out = jnp.dot(
            weights.astype(jnp.bfloat16), values_ref[:, cut], preferred_element_type=jnp.float32
        )
        parts.append((out / total).reshape(segment * SLOTS, GROUP, HEAD_SIZE))
        logs = jnp.where(lanes(logs.shape) == i * 2 + h, top * SCALE + jnp.log(total), logs)
    logs_ref[...] = logs.reshape(logs_ref.shape)
    both = jnp.concatenate(parts, axis=1).astype(jnp.bfloat16)
    part_ref[:, :, pair_rows(i), :] = both.reshape(segment, SLOTS, 16, HEAD_SIZE)


def kernel(
    segment,
    prompts_ref,
    length_ref,
    q_ref,
    key_ref,
    value_ref,
    own_keys_hbm,
    own_values_hbm,
    keys_hbm,
    values_hbm,
    weight_hbm,
    out_ref,
    own_keys,
    own_values,
    keys,
    values,
    weight,
    q_column,
    q_all,
    suffix,
    suffix_logs,
    parts,
    logs,
    got,
    got_logs,
    column,
    column_logs,
    rows_all,
    rows_wide,
    panel,
    local_sems,
    sems,
    chunk_sems,
):
    z, j = place(segment)
    n = segment * PROMPT_COUNT
    greet(n)
    loads = [
        pltpu.make_async_copy(src, dst, local_sems.at[i])
        for i, (src, dst) in enumerate(
            (
                (own_keys_hbm, own_keys),
                (own_values_hbm, own_values),
                (keys_hbm, keys),
                (values_hbm, values),
                (weight_hbm, weight),
            )
        )
    ]
    for load in loads:
        load.start()

    flat = q_ref[...].astype(jnp.float32)
    q = jnp.concatenate(
        [flat[:, h * HEAD_SIZE : (h + 1) * HEAD_SIZE] for h in range(QUERY_HEADS)], axis=0
    )
    q_column[z] = q.astype(jnp.bfloat16)
    logs[...] = jnp.zeros_like(logs)
    prompts = [prompts_ref[b] for b in range(PROMPT_COUNT)]
    ranks = []
    for b in range(PROMPT_COUNT):
        rank = jnp.int32(0)
        for c in range(b):
            rank = rank + jnp.where(prompts[c] == prompts[b], 1, 0)
        ranks.append(rank)
    slot_block = []
    for s in range(SLOTS):
        block = jnp.int32(0)
        for b in range(PROMPT_COUNT):
            block = jnp.where((prompts[b] == z) & (ranks[b] == s), b, block)
        slot_block.append(block)

    greeted(n)
    ask = exchange(q_column, sems.at[0], segment, over="column")
    ask[0]()
    loads[0].wait()
    loads[1].wait()
    halves = []
    own_logs = jnp.zeros((GROUP, 128), jnp.float32)
    own = (length_ref[0], q, own_keys, own_values, key_ref, value_ref)
    part, own_logs = own_suffix(range(4), own_logs, *own)
    halves.append(part)
    ask[1]()
    for s in range(SLOTS):
        q_all[j, s] = pick(slot_block[s], [q_column[b] for b in range(PROMPT_COUNT)])

    def ask_plane(i):
        return exchange(q_all, chunk_sems.at[0, i], segment, rows=pair_rows(i))

    def answer(i):
        return exchange(got, chunk_sems.at[1, i], segment, source=parts, rows=pair_rows(i))

    pairs = KEY_VALUE_HEADS // 2
    half = pairs // 2

    def head_rows(c):
        return pl.ds(c * HALF_HEADS, HALF_HEADS)

    def answer_logs(c):
        return exchange(got_logs.at[c], sems.at[3 + c], segment, source=logs.at[c])

    def share(c):
        return exchange(column, sems.at[5 + c], segment, over="column", rows=head_rows(c))

    def share_logs(c):
        return exchange(column_logs.at[c], sems.at[7 + c], segment, over="column")

    def gather(c):
        return exchange(rows_all, sems.at[9 + c], segment, rows=head_rows(c))

    for i in range(pairs):
        ask_plane(i)[0]()
    part, own_logs = own_suffix(range(4, KEY_VALUE_HEADS), own_logs, *own)
    halves.append(part)
    suffix[z] = jnp.concatenate(halves, axis=0)
    suffix_logs[z] = own_logs
    tell = exchange(suffix, sems.at[1], segment, over="column")
    tell_logs = exchange(suffix_logs, sems.at[2], segment, over="column")
    tell[0]()
    tell_logs[0]()
    loads[2].wait()
    loads[3].wait()

    def work(i):
        c = i // half
        ask_plane(i)[1]()
        attend(i, segment, q_all, keys, values, parts, logs.at[c])
        answer(i)[0]()
        if i % half == half - 1:
            answer_logs(c)[0]()
            got_logs[c, j] = logs[c, j]
        got[j, :, pair_rows(i), :] = parts[j, :, pair_rows(i), :]

    def combine(c):
        answer_logs(c)[1]()
        all_logs = got_logs[c]
        best = jnp.max(all_logs, axis=0)
        weights = jnp.exp(all_logs - best[None])
        total = jnp.sum(weights, axis=0)
        weights = weights / total[None]
        column_logs[c, z] = best + jnp.log(total)
        share_logs(c)[0]()
        for pair in range(c * half, (c + 1) * half):
            answer(pair)[1]()
            for s in range(SLOTS):
                rows = slice(pair * 16, pair * 16 + 16)
                acc = jnp.zeros((16, HEAD_SIZE), jnp.float32)
                for i in range(segment):
                    w = spread(weights[i, s * GROUP : (s + 1) * GROUP], pair)
                    acc = acc + w * got[i, s, rows].astype(jnp.float32)
                column[z, s, rows] = acc.astype(jnp.bfloat16)
        share(c)[0]()

    def finish_rows(c):
        share_logs(c)[1]()
        share(c)[1]()
        for b in range(PROMPT_COUNT):
            at = prompts[b] * SLOTS + ranks[b]
            prompt_logs = pick(
                at,
                [
                    column_logs[c, p, s * GROUP : (s + 1) * GROUP]
                    for p in range(PROMPT_COUNT)
                    for s in range(SLOTS)
                ],
            )
            own_logs = suffix_logs[b]
            best = jnp.maximum(prompt_logs, own_logs)
            prompt_weight = jnp.exp(prompt_logs - best)
            own_weight = jnp.exp(own_logs - best)
            total = prompt_weight + own_weight
            prompt_weight = prompt_weight / total
            own_weight = own_weight / total
            for pair in range(c * half, (c + 1) * half):
                rows = slice(pair * 16, pair * 16 + 16)
                prompt = pick(
                    at, [column[i // SLOTS, i % SLOTS, rows] for i in range(PROMPT_COUNT * SLOTS)]
                )
                row = spread(prompt_weight, pair) * prompt.astype(jnp.float32)
                row = row + spread(own_weight, pair) * suffix[b, rows]
                rows_all[j, b, rows] = row.astype(jnp.bfloat16)
        gather(c)[0]()

    def project(c, acc):
        gather(c)[1]()

        def widen(i, carry):
            for b in range(PROMPT_COUNT):
                at = (b * segment + i) * QUERY_HEADS + c * HALF_HEADS
                rows_wide[pl.ds(pl.multiple_of(at, HALF_HEADS), HALF_HEADS), :] = rows_all[
                    i, b, head_rows(c), :
                ].astype(jnp.float32)
            return carry

        lax.fori_loop(0, segment, widen, 0)

        def some(i, acc):
            for pair in range(4):
                h = i * 8 + pair * 2
                both = [rows_wide[pl.ds(h + o, n, stride=QUERY_HEADS), :] for o in range(2)]
                left = jnp.concatenate(both, axis=1).astype(jnp.bfloat16)
                at = pl.multiple_of(h * HEAD_SIZE, 2 * HEAD_SIZE)
                right = weight[pl.ds(at, 2 * HEAD_SIZE), :]
                acc = acc + jnp.dot(left, right, preferred_element_type=jnp.float32)
            return acc

        return lax.fori_loop(c * HALF_HEADS // 8, (c + 1) * HALF_HEADS // 8, some, acc)

    work(0)
    work(1)
    work(2)
    combine(0)
    work(3)
    tell_logs[1]()
    tell[1]()
    finish_rows(0)
    combine(1)
    loads[4].wait()
    for group in (ask, tell, tell_logs, answer_logs(0), answer_logs(1), share_logs(0), share(0)):
        group[2]()
    for i in range(pairs):
        ask_plane(i)[2]()
        answer(i)[2]()
    finish_rows(1)
    acc = project(0, jnp.zeros((n, weight.shape[1]), jnp.float32))
    share_logs(1)[2]()
    share(1)[2]()
    acc = project(1, acc)
    for r in range(n):
        panel[r] = acc[r : r + 1]
    home = exchange(out_ref, sems.at[11], segment, source=panel, over="all")
    home[0]()
    me = lax.axis_index("seq")
    out_ref[me] = panel[me]
    gather(0)[2]()
    gather(1)[2]()
    home[1]()
    home[2]()


def body(
    queries,
    shared_prompt_keys,
    shared_prompt_values,
    private_cached_keys,
    private_cached_values,
    token_keys,
    token_values,
    suffix_lengths,
    block_prompts,
    out_weight,
):
    n = lax.axis_size("seq")
    segment = n // PROMPT_COUNT
    count, width = queries.shape
    assert count == 1 and block_prompts.shape[0] == PROMPT_COUNT
    heads, size = QUERY_HEADS, HEAD_SIZE
    columns = out_weight.shape[1]
    bf, f32 = jnp.bfloat16, jnp.float32
    own_keys, own_values = private_cached_keys[0], private_cached_values[0]
    out = pl.pallas_call(
        functools.partial(kernel, segment),
        out_shape=jax.ShapeDtypeStruct((n, 1, columns), f32),
        in_specs=[SMEM, SMEM] + [VMEM] * 3 + [ANY] * 5,
        out_specs=VMEM,
        scratch_shapes=[
            pltpu.VMEM(own_keys.shape, bf),
            pltpu.VMEM(own_values.shape, bf),
            pltpu.VMEM(shared_prompt_keys.shape, bf),
            pltpu.VMEM(shared_prompt_values.shape, bf),
            pltpu.VMEM(out_weight.shape, bf),
            pltpu.VMEM((PROMPT_COUNT, heads, size), bf),
            pltpu.VMEM((segment, SLOTS, heads, size), bf),
            pltpu.VMEM((PROMPT_COUNT, heads, size), f32),
            pltpu.VMEM((PROMPT_COUNT, GROUP, 128), f32),
            pltpu.VMEM((segment, SLOTS, heads, size), bf),
            pltpu.VMEM((2, segment, SLOTS * GROUP, 128), f32),
            pltpu.VMEM((segment, SLOTS, heads, size), bf),
            pltpu.VMEM((2, segment, SLOTS * GROUP, 128), f32),
            pltpu.VMEM((PROMPT_COUNT, SLOTS, heads, size), bf),
            pltpu.VMEM((2, PROMPT_COUNT, SLOTS * GROUP, 128), f32),
            pltpu.VMEM((segment, PROMPT_COUNT, heads, size), bf),
            pltpu.VMEM((n * heads, size), f32),
            pltpu.VMEM((n, 1, columns), f32),
            pltpu.SemaphoreType.DMA((5,)),
            pltpu.SemaphoreType.DMA((12, 2)),
            pltpu.SemaphoreType.DMA((2, KEY_VALUE_HEADS // 2, 2)),
        ],
        compiler_params=pltpu.CompilerParams(
            collective_id=0, has_side_effects=True, vmem_limit_bytes=56 << 20
        ),
    )(
        block_prompts,
        suffix_lengths,
        queries,
        token_keys,
        token_values,
        own_keys,
        own_values,
        shared_prompt_keys,
        shared_prompt_values,
        out_weight,
    )
    return out.reshape(1, width).astype(bf)


def solution(mesh):
    in_specs = (
        P(("groups", "seq"), None),
        P(("groups", "seq"), None),
        P(("groups", "seq"), None),
        P(("groups", "seq"), None, None),
        P(("groups", "seq"), None, None),
        P(("groups", "seq"), None),
        P(("groups", "seq"), None),
        P(("groups", "seq")),
        P("groups"),
        P(None, "seq"),
    )
    out_specs = P(("groups", "seq"), None)
    return jax.shard_map(body, mesh=mesh, in_specs=in_specs, out_specs=out_specs, check_vma=False)
```
